512 devices in a mesh: row: 16 (over y, core), col: 8 (over z), depth: 4 (over x).
Axes of the slice: x: 4, y: 8, z: 8, core: 2. Of those that a mesh axis runs over, the one named last changes fastest.
Arguments:
- density_tiles: bfloat16 [4, 16, 8, 4, 256, 256], P('depth', 'row', 'col'), may hold values from -0.75 to 0.75
- density_rows: int32 [4, 16, 8, 4], P('depth', 'row', 'col'), may hold values from 0 to 7, as said below
- square_tiles: bfloat16 [4, 16, 8, 2, 2, 256, 256], P('depth', 'row', 'col'), may hold values from -0.75 to 0.75
- square_cols: int32 [4, 16, 8, 2, 2], P('depth', 'row', 'col'), may hold values from 0 to 3, as said below
- keep_rows: int32 [16, 8, 12], P('row', 'col'), may hold values from 0 to 7, as said below
- keep_cols: int32 [16, 8, 12], P('row', 'col'), may hold values from 0 to 3
- square_kept: bfloat16 [16, 8, 12, 256, 256], P('row', 'col', 'depth'), may hold values from -3 to 3
Outputs:
- next_density: bfloat16 [16, 8, 12, 256, 256], P('row', 'col', 'depth')
The draws below stay inside these ranges and needn't reach their ends.
Inputs may be any that keep to these rules, and one draw needn't show every extreme that they name: density_rows are distinct within one tile. square_cols are distinct within one piece. The pairs (keep_rows, keep_cols) are distinct within one tile.
All inputs are finite; a program needn't handle non-finite values.
Results may differ from the reference program's by a relative error of at most 0.001.
Values may be sent and summed in bfloat16 or wider, within the bound.
No kernel may reach another device: no remote copies, remote signals or barrier semaphores. Data moves between devices by JAX's collectives and lax.ppermute only.
A program may use at most 64 MiB of HBM per device.

```python
import jax
import jax.numpy as jnp
from jax import lax

BLK = 256
SA = 4
SB = 2
SC = 12
MB = 8
NB = 4
PIECES = 2
N_ROW = 16
N_COL = 8
N_DEPTH = 4


def distinct_picks(key, count, total, pick):
    keys = jax.random.split(key, count)
    return jax.vmap(lambda single: jax.random.permutation(single, total)[:pick])(keys).astype(jnp.int32)


def kept_cells(key):
    return distinct_picks(jax.random.fold_in(key, 7), N_ROW * N_COL, MB * NB, SC).reshape(N_ROW, N_COL, SC)


def draw_density_rows(key, part):
    key = jax.random.fold_in(key, 1)
    return distinct_picks(key, N_DEPTH * N_ROW * N_COL, MB, SA).reshape(N_DEPTH, N_ROW, N_COL, SA)


def draw_square_cols(key, part):
    key = jax.random.fold_in(key, 2)
    return distinct_picks(key, N_DEPTH * N_ROW * N_COL * PIECES, NB, SB).reshape(N_DEPTH, N_ROW, N_COL, PIECES, SB)


def draw_keep_rows(key, part):
    return kept_cells(key) // NB


def draw_keep_cols(key, part):
    return kept_cells(key) % NB


def level_of(stream_key, extent, pieces, smallest, high):
    def one(axis_at, parts):
        steps = jax.random.uniform(jax.random.fold_in(jax.random.fold_in(stream_key, 6), axis_at), (parts,), jnp.float32, smallest / len(pieces), high / len(pieces))
        return jnp.repeat(jnp.exp(steps), extent[axis_at] // parts).reshape((-1,) + (1,) * (len(extent) - axis_at - 1))

    loudness = one(*pieces[0])
    for cut in pieces[1:]:
        loudness = loudness * one(*cut)
    return loudness


def normal_values(stream_key, dims, spread, bound, cuts=(), kind=jnp.bfloat16):
    array = spread * jax.random.normal(stream_key, dims, jnp.float32)
    if cuts:
        array = array * level_of(stream_key, dims, cuts, -0.22, 0.18)
    return jnp.clip(array, -bound, bound).astype(kind)


def setup_inputs(seed: int = 0) -> dict:
    seeds = jax.random.split(jax.random.key(seed), 8)
    return {
        "density_tiles": normal_values(seeds[0], (N_DEPTH, N_ROW, N_COL, SA, BLK, BLK), 0.125, 0.75, ((0, 4), (1, 16), (2, 8))),
        "density_rows": draw_density_rows(jax.random.fold_in(seeds[7], 71), 0),
        "square_tiles": normal_values(seeds[2], (N_DEPTH, N_ROW, N_COL, PIECES, SB, BLK, BLK), 0.125, 0.75, ((0, 4), (1, 16), (2, 8))),
        "square_cols": draw_square_cols(jax.random.fold_in(seeds[7], 71), 0),
        "keep_rows": draw_keep_rows(jax.random.fold_in(seeds[7], 71), 0),
        "keep_cols": draw_keep_cols(jax.random.fold_in(seeds[7], 71), 0),
        "square_kept": normal_values(seeds[6], (N_ROW, N_COL, SC, BLK, BLK), 0.5, 3.0, ((0, 16), (1, 8), (2, 4))),
    }


def reference(density_tiles, density_rows, square_tiles, square_cols, keep_rows, keep_cols, square_kept):
    def one_slot(flat):
        rr = flat // (N_COL * SC)
        cc = (flat // SC) % N_COL
        ss = flat % SC
        want_row = keep_rows[rr, cc, ss]
        want_col = keep_cols[rr, cc, ss]

        def add_term(step, total):
            layer = step // N_ROW
            inner = step % N_ROW
            holder = (inner - cc) % N_ROW
            hits_a = density_rows[layer, holder, cc] == want_row
            slot_a = jnp.argmax(hits_a.astype(jnp.int32))
            offset = (inner - rr) % N_ROW
            owner = offset % N_COL
            which = offset // N_COL
            hits_b = square_cols[layer, rr, owner, which] == want_col
            slot_b = jnp.argmax(hits_b.astype(jnp.int32))
            present = jnp.any(hits_a) & jnp.any(hits_b)

            def multiply(value):
                return value + jnp.dot(density_tiles[layer, holder, cc, slot_a], square_tiles[layer, rr, owner, which, slot_b], preferred_element_type=jnp.float32)

            return lax.cond(present, multiply, lambda value: value, total)

        return lax.fori_loop(0, N_DEPTH * N_ROW, add_term, jnp.zeros((BLK, BLK), jnp.float32))

    cube = lax.map(one_slot, jnp.arange(N_ROW * N_COL * SC, dtype=jnp.int32))
    cube = cube.reshape(N_ROW, N_COL, SC, BLK, BLK)
    return (3.0 * square_kept.astype(jnp.float32) - 2.0 * cube).astype(jnp.bfloat16)
```

```python
import functools

import jax
import jax.numpy as jnp
from jax import lax
from jax.experimental import pallas as pl
from jax.experimental.pallas import tpu as pltpu
from jax.sharding import PartitionSpec as P

GROUP = 4
LEVELS = 32000.0
FINER = 16.0


def lists_kernel(steps, slots, place, rows_all, cols_all, want_rows, want_cols, list_a, list_b, counts, kept):
    held_a, held_b, pieces, tile_rows, tile_cols, owners = steps
    holders = owners * pieces
    my_row, my_col = place[0], place[1]

    def clear(index, carry):
        kept[index] = -1
        return carry

    lax.fori_loop(0, tile_rows * tile_cols, clear, 0)

    def mark(slot, carry):
        kept[want_rows[slot] * tile_cols + want_cols[slot]] = slot
        counts[slot] = 0
        return carry

    lax.fori_loop(0, slots, mark, 0)

    def blank(index, carry):
        list_a[index] = holders * held_a
        list_b[index] = 0
        return carry

    lax.fori_loop(0, slots * holders, blank, 0)

    def visit(step, carry):
        apart = step // pieces
        piece = step % pieces
        owner = lax.rem(my_col + apart, owners)
        holder = lax.rem(my_row + owner - my_col + piece * owners + holders, holders)
        for a in range(held_a):
            row = rows_all[holder * held_a + a]
            for b in range(held_b):
                col = cols_all[(owner * pieces + piece) * held_b + b]
                slot = kept[row * tile_cols + col]

                @pl.when(slot >= 0)
                def _():
                    count = counts[slot]
                    list_a[slot * holders + count] = holder * held_a + a
                    list_b[slot * holders + count] = step * held_b + b
                    counts[slot] = count + 1

        return carry

    lax.fori_loop(0, holders, visit, 0)


def product_kernel(slots, holders, shares, list_a, list_b, counts, a_all, *rest):
    parts, (coded, total, a_here, b_here, a_sem, b_sem) = rest[:-6], rest[-6:]
    blk = a_all.shape[1]
    each = slots // shares
    count_a = a_all.shape[0]
    copy_a = pltpu.make_async_copy(a_all, a_here.at[pl.ds(0, count_a)], a_sem)
    copy_a.start()
    copies = []
    at = 0
    for index, part in enumerate(parts):
        size = part.shape[0]
        copies.append(pltpu.make_async_copy(part, b_here.at[pl.ds(at, size)], b_sem.at[index]))
        copies[-1].start()
        at += size
    a_here[count_a] = jnp.zeros(a_here.shape[1:], a_here.dtype)
    for copy in copies:
        copy.wait()
    copy_a.wait()

    def grouped(slot, group):
        first = slot * holders + group * GROUP
        left = jnp.concatenate([a_here[list_a[first + n]] for n in range(GROUP)], axis=1)
        right = jnp.concatenate([b_here[list_b[first + n]] for n in range(GROUP)], axis=0)
        return jnp.dot(left, right, preferred_element_type=jnp.float32)

    def one_slot(slot, carry):
        total[...] = grouped(slot, 0)

        def one_group(group, inner):
            total[...] += grouped(slot, group)
            return inner

        lax.fori_loop(1, (counts[slot] + GROUP - 1) // GROUP, one_group, 0)
        largest = jnp.maximum(jnp.max(jnp.abs(total[...]), axis=0, keepdims=True), 1e-30)
        power = jnp.ceil(FINER * jnp.log2(largest / LEVELS))
        share, inside = slot // each, lax.rem(slot, each)
        values = jnp.round(total[...] * jnp.exp2(power * (-1.0 / FINER)))
        coded[share, pl.ds(pl.multiple_of(inside * blk, blk), blk), :] = values.astype(jnp.int32).astype(jnp.int16)
        powers = jnp.broadcast_to(power, (16, blk)).astype(jnp.int32).astype(jnp.int16)
        coded[share, pl.ds(pl.multiple_of(each * blk + inside * 16, 16), 16), :] = powers
        return carry

    lax.fori_loop(0, slots, one_slot, 0)


def finish_kernel(coded, square_kept, out):
    shares = coded.shape[0]
    each, blk = square_kept.shape[0], square_kept.shape[1]
    for slot in range(each):
        cube = jnp.zeros((blk, blk), jnp.float32)
        for share in range(shares):
            power = coded[share, pl.ds(each * blk + slot * 16, 16), :].astype(jnp.int32).astype(jnp.float32)[:1]
            values = coded[share, pl.ds(slot * blk, blk), :].astype(jnp.int32).astype(jnp.float32)
            cube = cube + values * jnp.exp2(power * (1.0 / FINER))
        out[slot] = (3.0 * square_kept[slot].astype(jnp.float32) - 2.0 * cube).astype(out.dtype)


def shifted(value, axis, steps):
    count = lax.axis_size(axis)
    return lax.ppermute(value, axis, [(source, (source + steps) % count) for source in range(count)])


def body(density_tiles, density_rows, square_tiles, square_cols, keep_rows, keep_cols, square_kept):
    n_row, n_col, n_depth = lax.axis_size("row"), lax.axis_size("col"), lax.axis_size("depth")
    tile_a = density_tiles[0, 0, 0]
    pieces, held_b, blk = square_tiles.shape[3], square_tiles.shape[4], square_tiles.shape[5]
    held_a = tile_a.shape[0]
    tile_b = square_tiles[0, 0, 0].reshape(pieces * held_b, blk, blk)
    slots = keep_rows.shape[-1]
    half = n_col // 2
    cut = tile_b.shape[0] // 2

    a_all = lax.all_gather(tile_a, "row", axis=0, tiled=True)

    my_rows, my_cols = density_rows[0, 0, 0], square_cols[0, 0, 0].reshape(-1)
    rows_all = lax.all_to_all(jnp.tile(my_rows, (n_row, 1)), "row", 0, 0, tiled=True).reshape(-1)
    cols_all = lax.all_to_all(jnp.tile(my_cols, (n_col, 1)), "col", 0, 0, tiled=True).reshape(-1)

    up = [tile_b]
    down = [tile_b]
    for step in range(1, half + 1):
        send_up, send_down = up[-1], down[-1]
        if step == 2:
            send_up, send_down, rows_all = lax.optimization_barrier((send_up, send_down, rows_all))
        if step == 3:
            send_up, send_down, cols_all = lax.optimization_barrier((send_up, send_down, cols_all))
        if step == half:
            send_up, send_down = send_up[:cut], send_down[cut:]
        up.append(shifted(send_up, "col", 1))
        down.append(shifted(send_down, "col", -1))
    parts = down[:half] + [up[half], down[half]] + up[1:half][::-1]

    place = jnp.stack([lax.axis_index("row"), lax.axis_index("col")]).astype(jnp.int32)

    tile_rows, tile_cols = 8, 4
    smem = pl.BlockSpec(memory_space=pltpu.SMEM)
    steps = (held_a, held_b, pieces, tile_rows, tile_cols, n_col)
    list_a, list_b, counts = pl.pallas_call(
        functools.partial(lists_kernel, steps, slots),
        out_shape=[
            jax.ShapeDtypeStruct((slots * n_row,), jnp.int32),
            jax.ShapeDtypeStruct((slots * n_row,), jnp.int32),
            jax.ShapeDtypeStruct((slots,), jnp.int32),
        ],
        in_specs=[smem] * 5,
        out_specs=[smem] * 3,
        scratch_shapes=[pltpu.SMEM((tile_rows * tile_cols,), jnp.int32)],
        name="lists",
    )(place, rows_all, cols_all, keep_rows[0, 0], keep_cols[0, 0])

    each = slots // n_depth
    coded = pl.pallas_call(
        functools.partial(product_kernel, slots, n_row, n_depth),
        out_shape=jax.ShapeDtypeStruct((n_depth, each * (blk + 16), blk), jnp.int16),
        in_specs=[smem] * 3 + [pl.BlockSpec(memory_space=pl.ANY)] * (1 + len(parts)),
        out_specs=pl.BlockSpec(memory_space=pltpu.VMEM),
        scratch_shapes=[
            pltpu.VMEM((blk, blk), jnp.float32),
            pltpu.VMEM((n_row * held_a + 1, blk, blk), jnp.bfloat16),
            pltpu.VMEM((n_col * pieces * held_b, blk, blk), jnp.bfloat16),
            pltpu.SemaphoreType.DMA,
            pltpu.SemaphoreType.DMA((len(parts),)),
        ],
        compiler_params=pltpu.CompilerParams(vmem_limit_bytes=60 * 1024 * 1024),
        cost_estimate=pl.CostEstimate(flops=2 * 64 * blk**3, bytes_accessed=16 * 2**20, transcendentals=0),
        name="products",
    )(list_a, list_b, counts, a_all, *parts)

    coded = lax.all_to_all(coded, "depth", 0, 0, tiled=True)
    result = pl.pallas_call(
        finish_kernel,
        out_shape=jax.ShapeDtypeStruct((each, blk, blk), jnp.bfloat16),
        compiler_params=pltpu.CompilerParams(vmem_limit_bytes=32 * 1024 * 1024),
        cost_estimate=pl.CostEstimate(flops=2**21, bytes_accessed=3 * 2**20, transcendentals=0),
        name="finish",
    )(coded, square_kept[0, 0])
    return result[None, None]


def solution(mesh):
    placed = (
        P("depth", "row", "col", None, None, None),
        P("depth", "row", "col", None),
        P("depth", "row", "col", None, None, None, None),
        P("depth", "row", "col", None, None),
        P("row", "col", None),
        P("row", "col", None),
        P("row", "col", "depth", None, None),
    )
    return jax.shard_map(
        body,
        mesh=mesh,
        in_specs=placed,
        out_specs=P("row", "col", "depth", None, None),
        check_vma=False,
    )
```

```python
import functools

import jax
import jax.numpy as jnp
from jax import lax
from jax.experimental import pallas as pl
from jax.experimental.pallas import tpu as pltpu
from jax.sharding import PartitionSpec as P

GROUP = 4
LEVELS = 32000.0
FINER = 16.0
PAD = 16
VMEM_BYTES = 28 * 1024 * 1024
LANES = 128


def prepare_kernel(sizes, place, rows, cols, tile_a, tile_b, out_a, out_b):
    held_a, held_b, blk, cut, owners = sizes
    whole_a, piece = held_a * blk, held_b * blk
    my_row, my_col = place[0], place[1]
    out_a[pl.ds(0, whole_a), :] = tile_a[...]
    out_b[pl.ds(0, piece), :] = tile_b[pl.ds(0, piece), :]
    out_b[pl.ds(cut, piece), :] = tile_b[pl.ds(piece, piece), :]
    lane = lax.broadcasted_iota(jnp.int32, (PAD, blk), 1) & (LANES // 2 - 1)
    spread = jnp.zeros((PAD, blk), jnp.int32)
    for a in range(held_a):
        spread = jnp.where(lane == my_row * held_a + a, rows[a] + 1, spread)
    out_a[pl.ds(whole_a, PAD), :] = spread.astype(jnp.float32).astype(out_a.dtype)
    spread = jnp.zeros((PAD, blk), jnp.int32)
    for index in range(cols.shape[0]):
        first = (my_col + index // held_b * owners) * held_a + index % held_b
        spread = jnp.where(lane == first, cols[index] + 1, spread)
    out_b[pl.ds(piece, PAD), :] = spread.astype(jnp.float32).astype(out_b.dtype)


def listed(rows_seen, cols_seen, keep_rows, keep_cols, my_row, my_col, sizes):
    slots, held_a, held_b, holders, owners = sizes
    lane = lax.broadcasted_iota(jnp.int32, (LANES, LANES), 0)
    holder = lax.broadcasted_iota(jnp.int32, (LANES, LANES), 1)
    mine = (lane < holders * held_a) & ((lane // held_a) == holder)
    pick_a = jnp.where(mine, lane + 1, 0)
    apart = (holder - my_row + holders) & (owners - 1)
    piece = ((holder + my_col - my_row + holders) & (holders - 1)) // owners
    pick_b = jnp.where(mine, (apart * 2 + piece) * held_b + (lane & (held_a - 1)) + 1, 0)
    before = jnp.where(lane <= holder, 1, 0)

    def numbers(seen, wanted, pick):
        sublane = lax.broadcasted_iota(jnp.int32, seen.shape, 0)
        target = jnp.full(seen.shape, -1, jnp.int32)
        for slot in range(slots):
            target = jnp.where(sublane == slot, wanted[slot] + 1, target)
        hits = jnp.where(seen == target.astype(jnp.float32), 1.0, 0.0).astype(jnp.bfloat16)
        pick = pick.astype(jnp.float32).astype(jnp.bfloat16)
        return jnp.dot(hits, pick, preferred_element_type=jnp.float32)

    number_a = numbers(rows_seen, keep_rows, pick_a)
    number_b = numbers(cols_seen, keep_cols, pick_b)
    both = jnp.where((number_a > 0) & (number_b > 0), 1.0, 0.0)
    before = before.astype(jnp.float32).astype(jnp.bfloat16)
    place = jnp.dot(both.astype(jnp.bfloat16), before, preferred_element_type=jnp.float32)
    code = (number_a - 1.0) + 128.0 * (number_b - 1.0)
    lane = lax.broadcasted_iota(jnp.int32, both.shape, 1)
    count = jnp.sum(both, axis=1, keepdims=True)
    result = jnp.where(lane == LANES - 1, count, 0.0)
    nothing = 128.0 * owners * 2 * held_b
    for at in range(holders):
        value = jnp.sum(jnp.where(place == at + 1.0, both * code, 0.0), axis=1, keepdims=True)
        result = jnp.where(lane == at, jnp.where(count > at, value, nothing), result)
    return result.astype(jnp.int32)


def multiply(sizes, lists, a_all, b_all, first, total):
    held_a, held_b, blk, cut = sizes

    def block_a(code):
        number = code & 127
        return a_all[number // held_a, pl.ds(pl.multiple_of(lax.rem(number, held_a) * blk, blk), blk), :]

    def block_b(code):
        number = code >> 7
        piece, inside = lax.rem(number // held_b, 2), lax.rem(number, held_b)
        return b_all[number // (2 * held_b), pl.ds(pl.multiple_of(piece * cut + inside * blk, PAD), blk), :]

    def grouped(slot, group):
        codes = [lists[slot, group * GROUP + n] for n in range(GROUP)]
        left = jnp.concatenate([block_a(code) for code in codes], axis=1)
        right = jnp.concatenate([block_b(code) for code in codes], axis=0)
        return jnp.dot(left, right, preferred_element_type=jnp.float32)

    count = total.shape[0]
    for index in range(count):
        total[index] = grouped(first + index, 0)
    for index in range(count):
        slot = first + index

        def one_group(group, carry, index=index, slot=slot):
            total[index] += grouped(slot, group)
            return carry

        lax.fori_loop(1, (lists[slot, LANES - 1] + GROUP - 1) // GROUP, one_group, 0)


def encode(total, index, coded, inside, blk, each):
    largest = jnp.maximum(jnp.max(jnp.abs(total[index]), axis=0, keepdims=True), 1e-30)
    power = jnp.ceil(FINER * jnp.log2(largest / LEVELS))
    values = jnp.round(total[index] * jnp.exp2(power * (-1.0 / FINER)))
    coded[pl.ds(inside * blk, blk), :] = values.astype(jnp.int32).astype(jnp.int16)
    powers = jnp.broadcast_to(power, (PAD, blk)).astype(jnp.int32).astype(jnp.int16)
    coded[pl.ds(each * blk + inside * PAD, PAD), :] = powers


def target(place, steps, shares, each):
    return lax.rem(place[2] + steps, shares) * each


def far_kernel(sizes, shares, place, keep_rows, keep_cols, a_all, *rest):
    parts, (coded, lists, b_all, total, scalar, sem) = rest[:-6], rest[-6:]
    held_a, held_b, blk, cut = sizes
    holders, owners, slots = a_all.shape[0], b_all.shape[0] - 1, keep_rows.shape[0]
    each = slots // shares
    my_row, my_col = place[0], place[1]
    for part, (owner, first) in zip(parts, rows_of(owners, cut)):
        b_all[owner, pl.ds(first, part.shape[0]), :] = part[...]
    b_all[owners, pl.ds(0, blk), :] = jnp.zeros((blk, blk), b_all.dtype)
    rows_seen = jnp.sum(a_all[:, pl.ds(held_a * blk, PAD), pl.ds(0, LANES)].astype(jnp.float32), axis=0)
    cols_seen = jnp.sum(b_all[pl.ds(0, owners), pl.ds(cut - PAD, PAD), pl.ds(0, LANES)].astype(jnp.float32), axis=0)
    turn = (my_row - my_col + holders) & (holders - 1)
    cols_seen = pltpu.roll(cols_seen, turn * held_a, 1)
    lists[...] = listed(
        rows_seen, cols_seen, keep_rows, keep_cols, my_row, my_col, (slots, held_a, held_b, holders, owners)
    )
    copy = pltpu.make_async_copy(lists, scalar, sem)
    copy.start()
    copy.wait()
    multiply(sizes, scalar, a_all, b_all, target(place, 2, shares, each), total)
    for index in range(each):
        encode(total, index, coded, index, blk, each)


def near_kernel(sizes, shares, each, place, lists, a_all, b_all, coded_up, coded_down, total_up, total_down):
    blk = sizes[2]
    multiply(sizes, lists, a_all, b_all, target(place, 1, shares, each), total_up)
    multiply(sizes, lists, a_all, b_all, target(place, shares - 1, shares, each), total_down)
    for index in range(each):
        encode(total_up, index, coded_up, index, blk, each)
        encode(total_down, index, coded_down, index, blk, each)


def own_kernel(sizes, shares, each, place, lists, a_all, b_all, total):
    multiply(sizes, lists, a_all, b_all, target(place, 0, shares, each), total)


def finish_kernel(far, up, down, own, square_kept, out):
    each, blk = square_kept.shape[0], square_kept.shape[1]
    for slot in range(each):
        cube = own[slot]
        for coded in (far, up, down):
            power = coded[pl.ds(each * blk + slot * PAD, PAD), :].astype(jnp.int32).astype(jnp.float32)[:1]
            values = coded[pl.ds(slot * blk, blk), :].astype(jnp.int32).astype(jnp.float32)
            cube = cube + values * jnp.exp2(power * (1.0 / FINER))
        out[slot] = (3.0 * square_kept[slot].astype(jnp.float32) - 2.0 * cube).astype(out.dtype)


def rows_of(owners, cut):
    half = owners // 2
    return [(apart, 0) for apart in range(half)] + [(half, 0), (half, cut)] + [(apart, 0) for apart in range(half + 1, owners)]


def shifted(value, axis, steps):
    count = lax.axis_size(axis)
    return lax.ppermute(value, axis, [(source, (source + steps) % count) for source in range(count)])


def body(density_tiles, density_rows, square_tiles, square_cols, keep_rows, keep_cols, square_kept):
    n_row, n_col, n_depth = lax.axis_size("row"), lax.axis_size("col"), lax.axis_size("depth")
    my_row, my_col = lax.axis_index("row"), lax.axis_index("col")
    held_a, blk = density_tiles.shape[3], density_tiles.shape[4]
    pieces, held_b = square_tiles.shape[3], square_tiles.shape[4]
    slots = keep_rows.shape[-1]
    half = n_col // 2
    cut = held_b * blk + PAD
    place = jnp.stack([my_row, my_col, lax.axis_index("depth")]).astype(jnp.int32)
    smem = pl.BlockSpec(memory_space=pltpu.SMEM)
    whole = pl.BlockSpec(memory_space=pltpu.VMEM)
    params = pltpu.CompilerParams(vmem_limit_bytes=VMEM_BYTES)
    tile_a, tile_b = pl.pallas_call(
        functools.partial(prepare_kernel, (held_a, held_b, blk, cut, n_col)),
        out_shape=[
            jax.ShapeDtypeStruct((held_a * blk + PAD, blk), jnp.bfloat16),
            jax.ShapeDtypeStruct((cut + held_b * blk, blk), jnp.bfloat16),
        ],
        in_specs=[smem] * 3 + [whole] * 2,
        out_specs=[whole] * 2,
        compiler_params=params,
        name="prepare",
    )(
        place,
        density_rows[0, 0, 0],
        square_cols[0, 0, 0].reshape(-1),
        density_tiles[0, 0, 0].reshape(held_a * blk, blk),
        square_tiles[0, 0, 0].reshape(pieces * held_b * blk, blk),
    )
    a_all = lax.all_gather(tile_a, "row")

    up, down = [tile_b], [tile_b]
    for step in range(1, half + 1):
        send_up, send_down = up[-1], down[-1]
        if step == half:
            send_up, send_down = send_up[:cut], send_down[cut:]
        up.append(shifted(send_up, "col", 1))
        down.append(shifted(send_down, "col", -1))
    parts = down[:half] + [up[half], down[half]] + up[1:half][::-1]

    each = slots // n_depth
    sizes = (held_a, held_b, blk, cut)
    coded = jax.ShapeDtypeStruct((each * (blk + PAD), blk), jnp.int16)
    summed = (each, blk, blk)

    def cost(count):
        return pl.CostEstimate(flops=8 * count * blk**3, bytes_accessed=count * 2**20, transcendentals=0)

    far, lists, b_all = pl.pallas_call(
        functools.partial(far_kernel, sizes, n_depth),
        out_shape=[
            coded,
            jax.ShapeDtypeStruct((PAD, LANES), jnp.int32),
            jax.ShapeDtypeStruct((n_col + 1, cut + held_b * blk, blk), jnp.bfloat16),
        ],
        in_specs=[smem] * 3 + [whole] * (1 + len(parts)),
        out_specs=[whole] * 3,
        scratch_shapes=[
            pltpu.VMEM(summed, jnp.float32),
            pltpu.SMEM((PAD, LANES), jnp.int32),
            pltpu.SemaphoreType.DMA,
        ],
        compiler_params=params,
        cost_estimate=cost(each),
        name="far",
    )(place, keep_rows[0, 0], keep_cols[0, 0], a_all, *parts)
    far = shifted(far, "depth", 2)
    up, down = pl.pallas_call(
        functools.partial(near_kernel, sizes, n_depth, each),
        out_shape=[coded] * 2,
        in_specs=[smem] * 2 + [whole] * 2,
        out_specs=[whole] * 2,
        scratch_shapes=[pltpu.VMEM(summed, jnp.float32)] * 2,
        compiler_params=params,
        cost_estimate=cost(2 * each),
        name="near",
    )(place, lists, a_all, b_all)
    up = shifted(up, "depth", 1)
    down = shifted(down, "depth", -1)
    own = pl.pallas_call(
        functools.partial(own_kernel, sizes, n_depth, each),
        out_shape=jax.ShapeDtypeStruct(summed, jnp.float32),
        in_specs=[smem] * 2 + [whole] * 2,
        out_specs=whole,
        compiler_params=params,
        cost_estimate=cost(each),
        name="own",
    )(place, lists, a_all, b_all)
    result = pl.pallas_call(
        finish_kernel,
        out_shape=jax.ShapeDtypeStruct(summed, jnp.bfloat16),
        compiler_params=params,
        cost_estimate=pl.CostEstimate(flops=2**21, bytes_accessed=3 * 2**20, transcendentals=0),
        name="finish",
    )(far, up, down, own, square_kept[0, 0])
    return result[None, None]


def solution(mesh):
    placed = (
        P("depth", "row", "col", None, None, None),
        P("depth", "row", "col", None),
        P("depth", "row", "col", None, None, None, None),
        P("depth", "row", "col", None, None),
        P("row", "col", None),
        P("row", "col", None),
        P("row", "col", "depth", None, None),
    )
    return jax.shard_map(
        body,
        mesh=mesh,
        in_specs=placed,
        out_specs=P("row", "col", "depth", None, None),
        check_vma=False,
    )
```

```python
import functools

import jax
import jax.numpy as jnp
from jax import lax
from jax.experimental import pallas as pl
from jax.experimental.pallas import tpu as pltpu
from jax.sharding import PartitionSpec as P

GROUP = 4
LEVELS = 32000.0
FINER = 16.0
PAD = 16
VMEM_BYTES = 18 * 1024 * 1024
CORES = 2
LANES = 128


def prepare_kernel(sizes, place, rows, cols, tile_a, tile_b, out_a, out_b, sems):
    held_a, held_b, blk, cut, owners = sizes
    whole_a, piece = held_a * blk, held_b * blk
    my_row, my_col = place[0], place[1]
    copies = [
        pltpu.make_async_copy(tile_a, out_a.at[pl.ds(0, whole_a), :], sems.at[0]),
        pltpu.make_async_copy(tile_b.at[pl.ds(0, piece), :], out_b.at[pl.ds(0, piece), :], sems.at[1]),
        pltpu.make_async_copy(tile_b.at[pl.ds(piece, piece), :], out_b.at[pl.ds(cut, piece), :], sems.at[2]),
    ]
    for copy in copies:
        copy.start()
    lane = lax.broadcasted_iota(jnp.int32, (PAD, blk), 1) & (LANES // 2 - 1)
    spread = jnp.zeros((PAD, blk), jnp.int32)
    for a in range(held_a):
        spread = jnp.where(lane == my_row * held_a + a, rows[a] + 1, spread)
    out_a[pl.ds(whole_a, PAD), :] = spread.astype(jnp.float32).astype(out_a.dtype)
    spread = jnp.zeros((PAD, blk), jnp.int32)
    for index in range(2 * held_b):
        first = (my_col + index // held_b * owners) * held_a + index % held_b
        spread = jnp.where(lane == first, cols[index // held_b, index % held_b] + 1, spread)
    out_b[pl.ds(piece, PAD), :] = spread.astype(jnp.float32).astype(out_b.dtype)
    for copy in copies:
        copy.wait()


def turned(distance, forward, count):
    distance = jnp.where(forward, distance, count - distance) & (count - 1)
    rank = jnp.zeros_like(distance)
    for place, steps in enumerate(arrivals(count)):
        rank = jnp.where(distance == steps % count, place, rank)
    return rank


def arrivals(count):
    order, low, high = [0, 1], 0, 1
    while len(order) < count:
        order += [low - 1, low - 2]
        low -= 2
        if len(order) < count:
            order += [high + 1, high + 2]
            high += 2
    return order


def starts_forward(core, position):
    return lax.rem(core + position, 2) == 0


def listed(rows_seen, cols_seen, keep_rows, keep_cols, my_row, my_col, sizes):
    slots, held_a, held_b, holders, owners = sizes
    chips = holders // CORES
    my_core, my_chip = lax.rem(my_row, CORES), my_row // CORES
    holder = lax.broadcasted_iota(jnp.int32, (8, LANES), 1)
    core, chip = holder & (CORES - 1), (holder // CORES) & (chips - 1)
    forward = ((core + my_chip) & 1) == 0
    rank_a = turned((chip - my_chip + chips) & (chips - 1), forward, chips)
    rank_a = rank_a + jnp.where(core == my_core, 0, chips)
    offset = (holder + my_col - my_row + holders) & (holders - 1)
    owner, piece = offset & (owners - 1), offset // owners
    rank_b = turned((owner - my_col + owners) & (owners - 1), starts_forward(my_core, my_col), owners)
    rank_a, rank_b = rank_a[:1] * held_a, ((rank_b * 2 + piece) * held_b)[:1]
    lane = lax.broadcasted_iota(jnp.int32, (LANES, LANES), 0)
    holder = lax.broadcasted_iota(jnp.int32, (LANES, LANES), 1)
    mine = (lane < holders * held_a) & ((lane // held_a) == holder)
    pick_a = jnp.where(mine, rank_a + (lane & (held_a - 1)) + 1, 0)
    pick_b = jnp.where(mine, rank_b + (lane & (held_a - 1)) + 1, 0)
    before = jnp.where(lane <= holder, 1, 0)

    def numbers(seen, wanted, pick):
        sublane = lax.broadcasted_iota(jnp.int32, seen.shape, 0)
        target = jnp.full(seen.shape, -1, jnp.int32)
        for slot in range(slots):
            target = jnp.where(sublane == slot, wanted[slot] + 1, target)
        hits = jnp.where(seen == target.astype(jnp.float32), 1.0, 0.0).astype(jnp.bfloat16)
        pick = pick.astype(jnp.float32).astype(jnp.bfloat16)
        return jnp.dot(hits, pick, preferred_element_type=jnp.float32)

    number_a = numbers(rows_seen, keep_rows, pick_a)
    number_b = numbers(cols_seen, keep_cols, pick_b)
    both = jnp.where((number_a > 0) & (number_b > 0), 1.0, 0.0)
    before = before.astype(jnp.float32).astype(jnp.bfloat16)
    place = jnp.dot(both.astype(jnp.bfloat16), before, preferred_element_type=jnp.float32)
    code = (number_a - 1.0) + 128.0 * (number_b - 1.0)
    lane = lax.broadcasted_iota(jnp.int32, both.shape, 1)
    count = jnp.sum(both, axis=1, keepdims=True)
    result = jnp.where(lane == LANES - 1, count, 0.0)
    nothing = 128.0 * owners * 2 * held_b
    for at in range(holders):
        value = jnp.sum(jnp.where(place == at + 1.0, both * code, 0.0), axis=1, keepdims=True)
        result = jnp.where(lane == at, jnp.where(count > at, value, nothing), result)
    return result.astype(jnp.int32)


def multiply(sizes, lists, a_all, b_all, first, total):
    held_a, held_b, blk, cut = sizes

    def block_a(code):
        number = code & 127
        return a_all[number // held_a, pl.ds(pl.multiple_of(lax.rem(number, held_a) * blk, blk), blk), :]

    def block_b(code):
        number = code >> 7
        piece, inside = lax.rem(number // held_b, 2), lax.rem(number, held_b)
        return b_all[number // (2 * held_b), pl.ds(pl.multiple_of(piece * cut + inside * blk, PAD), blk), :]

    def grouped(slot, group):
        codes = [lists[slot, group * GROUP + n] for n in range(GROUP)]
        left = jnp.concatenate([block_a(code) for code in codes], axis=1)
        right = jnp.concatenate([block_b(code) for code in codes], axis=0)
        return jnp.dot(left, right, preferred_element_type=jnp.float32)

    count = total.shape[0]
    for index in range(count):
        total[index] = grouped(first + index, 0)
    for index in range(count):
        slot = first + index

        def one_group(group, carry, index=index, slot=slot):
            total[index] += grouped(slot, group)
            return carry

        lax.fori_loop(1, (lists[slot, LANES - 1] + GROUP - 1) // GROUP, one_group, 0)


def encode(total, index, coded, inside, blk, each):
    largest = jnp.maximum(jnp.max(jnp.abs(total[index]), axis=0, keepdims=True), 1e-30)
    power = jnp.ceil(FINER * jnp.log2(largest / LEVELS))
    values = jnp.round(total[index] * jnp.exp2(power * (-1.0 / FINER)))
    coded[pl.ds(inside * blk, blk), :] = values.astype(jnp.int32).astype(jnp.int16)
    powers = jnp.broadcast_to(power, (PAD, blk)).astype(jnp.int32).astype(jnp.int16)
    coded[pl.ds(each * blk + inside * PAD, PAD), :] = powers


def target(place, steps, shares, each):
    return lax.rem(place[2] + steps, shares) * each


def join_kernel(*refs):
    parts, whole = refs[:-1], refs[-1]
    at = 0
    for part in parts:
        size = part.shape[0]
        whole[pl.ds(at, size)] = part[...]
        at += size
    blk = whole.shape[2]
    whole[at, pl.ds(0, blk), :] = jnp.zeros((blk, blk), whole.dtype)


def far_kernel(sizes, shares, count_a, place, keep_rows, keep_cols, *rest):
    parts_a, b_all = rest[:count_a], rest[count_a]
    coded, lists, a_all, total, scalar, sem = rest[count_a + 1 :]
    held_a, held_b, blk, cut = sizes
    holders, owners, slots = a_all.shape[0], b_all.shape[0] - 1, keep_rows.shape[0]
    each = slots // shares
    my_row, my_col = place[0], place[1]
    at = 0
    for part in parts_a:
        size = part.shape[0]
        a_all[pl.ds(at, size)] = part[...]
        at += size
    rows_seen = jnp.sum(a_all[:, pl.ds(held_a * blk, PAD), pl.ds(0, LANES)].astype(jnp.float32), axis=0)
    cols_seen = jnp.sum(b_all[pl.ds(0, owners), pl.ds(cut - PAD, PAD), pl.ds(0, LANES)].astype(jnp.float32), axis=0)
    turn = (my_row - my_col + holders) & (holders - 1)
    cols_seen = pltpu.roll(cols_seen, turn * held_a, 1)
    lists[...] = listed(
        rows_seen, cols_seen, keep_rows, keep_cols, my_row, my_col, (slots, held_a, held_b, holders, owners)
    )
    copy = pltpu.make_async_copy(lists, scalar, sem)
    copy.start()
    copy.wait()
    multiply(sizes, scalar, a_all, b_all, target(place, 2, shares, each), total)
    for index in range(each):
        encode(total, index, coded, index, blk, each)


def near_kernel(sizes, shares, each, place, lists, a_all, b_all, coded_up, coded_down, total_up, total_down):
    blk = sizes[2]
    multiply(sizes, lists, a_all, b_all, target(place, 1, shares, each), total_up)
    multiply(sizes, lists, a_all, b_all, target(place, shares - 1, shares, each), total_down)
    for index in range(each):
        encode(total_up, index, coded_up, index, blk, each)
        encode(total_down, index, coded_down, index, blk, each)


def own_kernel(sizes, shares, each, place, lists, a_all, b_all, total):
    multiply(sizes, lists, a_all, b_all, target(place, 0, shares, each), total)


def finish_kernel(far, up, down, own, square_kept, out):
    each, blk = square_kept.shape[0], square_kept.shape[1]
    for slot in range(each):
        cube = own[slot]
        for coded in (far, up, down):
            power = coded[pl.ds(each * blk + slot * PAD, PAD), :].astype(jnp.int32).astype(jnp.float32)[:1]
            values = coded[pl.ds(slot * blk, blk), :].astype(jnp.int32).astype(jnp.float32)
            cube = cube + values * jnp.exp2(power * (1.0 / FINER))
        out[slot] = (3.0 * square_kept[slot].astype(jnp.float32) - 2.0 * cube).astype(out.dtype)


def exchanged(value, axes, sizes, axis, first):
    rows, cols = sizes
    pairs = []
    for row in range(rows):
        for col in range(cols):
            core, chip = row % CORES, row // CORES
            count, position = (rows // CORES, chip) if axis == "row" else (cols, col)
            forward = ((core + position) % 2 == 0) == first
            other = (position + (1 if forward else -1)) % count
            partner = (other * CORES + core, col) if axis == "row" else (row, other)
            pairs.append((row * cols + col, partner[0] * cols + partner[1]))
    return lax.ppermute(value, axes, pairs)


def shifted(value, axis, steps):
    count = lax.axis_size(axis)
    return lax.ppermute(value, axis, [(source, (source + steps) % count) for source in range(count)])


def siblings(value):
    count = lax.axis_size("row")
    return lax.ppermute(value, "row", [(source, source ^ 1) for source in range(count)])


def body(density_tiles, density_rows, square_tiles, square_cols, keep_rows, keep_cols, square_kept):
    n_row, n_col, n_depth = lax.axis_size("row"), lax.axis_size("col"), lax.axis_size("depth")
    my_row, my_col = lax.axis_index("row"), lax.axis_index("col")
    held_a, blk = density_tiles.shape[3], density_tiles.shape[4]
    pieces, held_b = square_tiles.shape[3], square_tiles.shape[4]
    slots = keep_rows.shape[-1]
    cut = held_b * blk + PAD
    place = jnp.stack([my_row, my_col, lax.axis_index("depth")]).astype(jnp.int32)
    smem = pl.BlockSpec(memory_space=pltpu.SMEM)
    whole = pl.BlockSpec(memory_space=pltpu.VMEM)
    params = pltpu.CompilerParams(vmem_limit_bytes=VMEM_BYTES)
    tile_a, tile_b = pl.pallas_call(
        functools.partial(prepare_kernel, (held_a, held_b, blk, cut, n_col)),
        out_shape=[
            jax.ShapeDtypeStruct((held_a * blk + PAD, blk), jnp.bfloat16),
            jax.ShapeDtypeStruct((cut + held_b * blk, blk), jnp.bfloat16),
        ],
        in_specs=[smem] * 3 + [pl.BlockSpec(memory_space=pl.ANY)] * 2,
        out_specs=[whole] * 2,
        scratch_shapes=[pltpu.SemaphoreType.DMA((3,))],
        compiler_params=pltpu.CompilerParams(vmem_limit_bytes=60 * 1024 * 1024),
        name="prepare",
    )(
        place,
        density_rows[0, 0, 0],
        square_cols[0, 0, 0],
        density_tiles[0, 0, 0].reshape(held_a * blk, blk),
        square_tiles[0, 0, 0].reshape(pieces * held_b * blk, blk),
    )
    tile_a, tile_b = tile_a[None], tile_b[None]

    def swap(value, axis, turn):
        return exchanged(value, ("row", "col"), (n_row, n_col), axis, turn % 2 == 0)

    def both(turn, pair):
        return [swap(pair[0], "row", turn), swap(pair[1], "col", turn)]

    tiles = (tile_a, tile_b)
    first = both(0, tiles)
    second = both(1, tiles)
    second = [jnp.concatenate(two) for two in zip(second, both(1, first))]
    third = both(0, second)
    fourth = both(1, third)
    from_sibling = [
        siblings(jnp.concatenate([tile_a, first[0], second[0]])),
        siblings(third[0]),
        siblings(fourth[0]),
    ]
    chain_a, chain_b = [list(parts) for parts in zip(tiles, first, second, third, fourth)]
    parts_a, parts_b = chain_a + from_sibling, chain_b

    each = slots // n_depth
    sizes = (held_a, held_b, blk, cut)
    coded = jax.ShapeDtypeStruct((each * (blk + PAD), blk), jnp.int16)
    summed = (each, blk, blk)

    def cost(count):
        return pl.CostEstimate(flops=8 * count * blk**3, bytes_accessed=count * 2**20, transcendentals=0)

    b_all = pl.pallas_call(
        join_kernel,
        out_shape=jax.ShapeDtypeStruct((n_col + 1, cut + held_b * blk, blk), jnp.bfloat16),
        in_specs=[whole] * len(parts_b),
        out_specs=whole,
        compiler_params=params,
        cost_estimate=pl.CostEstimate(flops=10 * 10**9, bytes_accessed=8 * 2**20, transcendentals=0),
        name="join",
    )(*parts_b)
    far, lists, a_all = pl.pallas_call(
        functools.partial(far_kernel, sizes, n_depth, len(parts_a)),
        out_shape=[
            coded,
            jax.ShapeDtypeStruct((PAD, LANES), jnp.int32),
            jax.ShapeDtypeStruct((n_row, held_a * blk + PAD, blk), jnp.bfloat16),
        ],
        in_specs=[smem] * 3 + [whole] * (len(parts_a) + 1),
        out_specs=[whole] * 3,
        scratch_shapes=[
            pltpu.VMEM(summed, jnp.float32),
            pltpu.SMEM((PAD, LANES), jnp.int32),
            pltpu.SemaphoreType.DMA,
        ],
        compiler_params=params,
        cost_estimate=cost(each),
        name="far",
    )(place, keep_rows[0, 0], keep_cols[0, 0], *parts_a, b_all)
    far = shifted(far, "depth", 2)
    up, down = pl.pallas_call(
        functools.partial(near_kernel, sizes, n_depth, each),
        out_shape=[coded] * 2,
        in_specs=[smem] * 2 + [whole] * 2,
        out_specs=[whole] * 2,
        scratch_shapes=[pltpu.VMEM(summed, jnp.float32)] * 2,
        compiler_params=params,
        cost_estimate=cost(2 * each),
        name="near",
    )(place, lists, a_all, b_all)
    up = shifted(up, "depth", 1)
    down = shifted(down, "depth", -1)
    own = pl.pallas_call(
        functools.partial(own_kernel, sizes, n_depth, each),
        out_shape=jax.ShapeDtypeStruct(summed, jnp.float32),
        in_specs=[smem] * 2 + [whole] * 2,
        out_specs=whole,
        compiler_params=params,
        cost_estimate=cost(each),
        name="own",
    )(place, lists, a_all, b_all)
    result = pl.pallas_call(
        finish_kernel,
        out_shape=jax.ShapeDtypeStruct(summed, jnp.bfloat16),
        compiler_params=params,
        cost_estimate=pl.CostEstimate(flops=2**21, bytes_accessed=3 * 2**20, transcendentals=0),
        name="finish",
    )(far, up, down, own, square_kept[0, 0])
    return result[None, None]


def solution(mesh):
    placed = (
        P("depth", "row", "col", None, None, None),
        P("depth", "row", "col", None),
        P("depth", "row", "col", None, None, None, None),
        P("depth", "row", "col", None, None),
        P("row", "col", None),
        P("row", "col", None),
        P("row", "col", "depth", None, None),
    )
    return jax.shard_map(
        body,
        mesh=mesh,
        in_specs=placed,
        out_specs=P("row", "col", "depth", None, None),
        check_vma=False,
    )
```

```python
import functools

import jax
import jax.numpy as jnp
from jax import lax
from jax.experimental import pallas as pl
from jax.experimental.pallas import tpu as pltpu
from jax.sharding import PartitionSpec as P

GROUP = 4
LEVELS = 32000.0
FINER = 16.0
PAD = 16
VMEM_BYTES = 18 * 1024 * 1024
CORES = 2
LANES = 128


def prepare_kernel(sizes, place, rows, cols, tile_a, tile_b, out_a, out_b, sems):
    held_a, held_b, blk, cut, owners = sizes
    whole_a, piece = held_a * blk, held_b * blk
    my_row, my_col = place[0], place[1]
    copies = [
        pltpu.make_async_copy(tile_a, out_a.at[pl.ds(0, whole_a), :], sems.at[0]),
        pltpu.make_async_copy(tile_b.at[pl.ds(0, piece), :], out_b.at[pl.ds(0, piece), :], sems.at[1]),
        pltpu.make_async_copy(tile_b.at[pl.ds(piece, piece), :], out_b.at[pl.ds(cut, piece), :], sems.at[2]),
    ]
    for copy in copies:
        copy.start()
    lane = lax.broadcasted_iota(jnp.int32, (PAD, blk), 1) & (LANES // 2 - 1)
    spread = jnp.zeros((PAD, blk), jnp.int32)
    for a in range(held_a):
        spread = jnp.where(lane == my_row * held_a + a, rows[a] + 1, spread)
    out_a[pl.ds(whole_a, PAD), :] = spread.astype(jnp.float32).astype(out_a.dtype)
    spread = jnp.zeros((PAD, blk), jnp.int32)
    for index in range(2 * held_b):
        first = (my_col + index // held_b * owners) * held_a + index % held_b
        spread = jnp.where(lane == first, cols[index // held_b, index % held_b] + 1, spread)
    out_b[pl.ds(piece, PAD), :] = spread.astype(jnp.float32).astype(out_b.dtype)
    for copy in copies:
        copy.wait()


def turned(distance, forward, count):
    distance = jnp.where(forward, distance, count - distance) & (count - 1)
    rank = jnp.zeros_like(distance)
    for place, steps in enumerate(arrivals(count)):
        rank = jnp.where(distance == steps % count, place, rank)
    return rank


def arrivals(count):
    order, low, high = [0, 1], 0, 1
    while len(order) < count:
        order += [low - 1, low - 2]
        low -= 2
        if len(order) < count:
            order += [high + 1, high + 2]
            high += 2
    return order


def starts_forward(core, position):
    return lax.rem(core + position, 2) == 0


def listed(rows_seen, cols_seen, keep_rows, keep_cols, my_row, my_col, sizes):
    slots, held_a, held_b, holders, owners = sizes
    chips = holders // CORES
    my_core, my_chip = lax.rem(my_row, CORES), my_row // CORES
    holder = lax.broadcasted_iota(jnp.int32, (8, LANES), 1)
    core, chip = holder & (CORES - 1), (holder // CORES) & (chips - 1)
    forward = ((core + my_chip) & 1) == 0
    rank_a = turned((chip - my_chip + chips) & (chips - 1), forward, chips)
    rank_a = rank_a + jnp.where(core == my_core, 0, chips)
    offset = (holder + my_col - my_row + holders) & (holders - 1)
    owner, piece = offset & (owners - 1), offset // owners
    rank_b = turned((owner - my_col + owners) & (owners - 1), starts_forward(my_core, my_col), owners)
    rank_a, rank_b = rank_a[:1] * held_a, ((rank_b * 2 + piece) * held_b)[:1]
    lane = lax.broadcasted_iota(jnp.int32, (LANES, LANES), 0)
    holder = lax.broadcasted_iota(jnp.int32, (LANES, LANES), 1)
    mine = (lane < holders * held_a) & ((lane // held_a) == holder)
    pick_a = jnp.where(mine, rank_a + (lane & (held_a - 1)) + 1, 0)
    pick_b = jnp.where(mine, rank_b + (lane & (held_a - 1)) + 1, 0)
    before = jnp.where(lane <= holder, 1, 0)

    def numbers(seen, wanted, pick):
        sublane = lax.broadcasted_iota(jnp.int32, seen.shape, 0)
        target = jnp.full(seen.shape, -1, jnp.int32)
        for slot in range(slots):
            target = jnp.where(sublane == slot, wanted[slot] + 1, target)
        hits = jnp.where(seen == target.astype(jnp.float32), 1.0, 0.0).astype(jnp.bfloat16)
        pick = pick.astype(jnp.float32).astype(jnp.bfloat16)
        return jnp.dot(hits, pick, preferred_element_type=jnp.float32)

    number_a = numbers(rows_seen, keep_rows, pick_a)
    number_b = numbers(cols_seen, keep_cols, pick_b)
    both = jnp.where((number_a > 0) & (number_b > 0), 1.0, 0.0)
    before = before.astype(jnp.float32).astype(jnp.bfloat16)
    place = jnp.dot(both.astype(jnp.bfloat16), before, preferred_element_type=jnp.float32)
    code = (number_a - 1.0) + 128.0 * (number_b - 1.0)
    lane = lax.broadcasted_iota(jnp.int32, both.shape, 1)
    count = jnp.sum(both, axis=1, keepdims=True)
    result = jnp.where(lane == LANES - 1, count, 0.0)
    nothing = 128.0 * owners * 2 * held_b
    for at in range(holders):
        value = jnp.sum(jnp.where(place == at + 1.0, both * code, 0.0), axis=1, keepdims=True)
        result = jnp.where(lane == at, jnp.where(count > at, value, nothing), result)
    return result.astype(jnp.int32)


def multiply(sizes, lists, a_all, b_all, first, total):
    held_a, held_b, blk, cut = sizes

    def block_a(code):
        number = code & 127
        return a_all[number // held_a, pl.ds(pl.multiple_of(lax.rem(number, held_a) * blk, blk), blk), :]

    def block_b(code):
        number = code >> 7
        piece, inside = lax.rem(number // held_b, 2), lax.rem(number, held_b)
        return b_all[number // (2 * held_b), pl.ds(pl.multiple_of(piece * cut + inside * blk, PAD), blk), :]

    def grouped(slot, group):
        codes = [lists[slot, group * GROUP + n] for n in range(GROUP)]
        left = jnp.concatenate([block_a(code) for code in codes], axis=1)
        right = jnp.concatenate([block_b(code) for code in codes], axis=0)
        return jnp.dot(left, right, preferred_element_type=jnp.float32)

    count = total.shape[0]
    for index in range(count):
        total[index] = grouped(first + index, 0)
    for index in range(count):
        slot = first + index

        def one_group(group, carry, index=index, slot=slot):
            total[index] += grouped(slot, group)
            return carry

        lax.fori_loop(1, (lists[slot, LANES - 1] + GROUP - 1) // GROUP, one_group, 0)


def encode(total, index, coded, inside, blk, each):
    largest = jnp.maximum(jnp.max(jnp.abs(total[index]), axis=0, keepdims=True), 1e-30)
    power = jnp.ceil(FINER * jnp.log2(largest / LEVELS))
    values = jnp.round(total[index] * jnp.exp2(power * (-1.0 / FINER)))
    coded[pl.ds(inside * blk, blk), :] = values.astype(jnp.int32).astype(jnp.int16)
    return power


def keep_powers(powers, coded, first):
    row = lax.broadcasted_iota(jnp.int32, (PAD, coded.shape[1]), 0)
    value = jnp.zeros(row.shape, jnp.float32)
    for index, power in enumerate(powers):
        value = jnp.where(row == index, power, value)
    coded[pl.ds(first, PAD), :] = value.astype(jnp.int32).astype(jnp.int16)


def target(place, steps, shares, each):
    return lax.rem(place[2] + steps, shares) * each


def join_kernel(*refs):
    parts, whole = refs[:-1], refs[-1]
    at = 0
    for part in parts:
        size = part.shape[0]
        whole[pl.ds(at, size)] = part[...]
        at += size
    blk = whole.shape[2]
    whole[at, pl.ds(0, blk), :] = jnp.zeros((blk, blk), whole.dtype)


def far_kernel(sizes, shares, count_a, place, keep_rows, keep_cols, *rest):
    parts_a, b_all = rest[:count_a], rest[count_a]
    coded, lists, a_all, total, scalar, sem = rest[count_a + 1 :]
    held_a, held_b, blk, cut = sizes
    holders, owners, slots = a_all.shape[0], b_all.shape[0] - 1, keep_rows.shape[0]
    each = slots // shares
    my_row, my_col = place[0], place[1]
    at = 0
    for part in parts_a:
        size = part.shape[0]
        a_all[pl.ds(at, size)] = part[...]
        at += size
    rows_seen = jnp.sum(a_all[:, pl.ds(held_a * blk, PAD), pl.ds(0, LANES)].astype(jnp.float32), axis=0)
    cols_seen = jnp.sum(b_all[pl.ds(0, owners), pl.ds(cut - PAD, PAD), pl.ds(0, LANES)].astype(jnp.float32), axis=0)
    turn = (my_row - my_col + holders) & (holders - 1)
    cols_seen = pltpu.roll(cols_seen, turn * held_a, 1)
    lists[...] = listed(
        rows_seen, cols_seen, keep_rows, keep_cols, my_row, my_col, (slots, held_a, held_b, holders, owners)
    )
    copy = pltpu.make_async_copy(lists, scalar, sem)
    copy.start()
    copy.wait()
    multiply(sizes, scalar, a_all, b_all, target(place, 2, shares, each), total)
    keep_powers([encode(total, index, coded, index, blk, each) for index in range(each)], coded, each * blk)


def near_kernel(sizes, shares, each, place, lists, a_all, b_all, coded_up, coded_down, total_up, total_down):
    blk = sizes[2]
    multiply(sizes, lists, a_all, b_all, target(place, 1, shares, each), total_up)
    multiply(sizes, lists, a_all, b_all, target(place, shares - 1, shares, each), total_down)
    for total, coded in ((total_up, coded_up), (total_down, coded_down)):
        keep_powers([encode(total, index, coded, index, blk, each) for index in range(each)], coded, each * blk)


def own_kernel(sizes, shares, each, place, lists, a_all, b_all, total):
    multiply(sizes, lists, a_all, b_all, target(place, 0, shares, each), total)


def finish_kernel(far, up, down, own, square_kept, out):
    each, blk = square_kept.shape[0], square_kept.shape[1]
    for slot in range(each):
        cube = own[slot]
        for coded in (far, up, down):
            power = coded[pl.ds(each * blk, PAD), :].astype(jnp.int32).astype(jnp.float32)[slot : slot + 1]
            values = coded[pl.ds(slot * blk, blk), :].astype(jnp.int32).astype(jnp.float32)
            cube = cube + values * jnp.exp2(power * (1.0 / FINER))
        out[slot] = (3.0 * square_kept[slot].astype(jnp.float32) - 2.0 * cube).astype(out.dtype)


def exchanged(value, axes, sizes, axis, first):
    rows, cols = sizes
    pairs = []
    for row in range(rows):
        for col in range(cols):
            core, chip = row % CORES, row // CORES
            count, position = (rows // CORES, chip) if axis == "row" else (cols, col)
            forward = ((core + position) % 2 == 0) == first
            other = (position + (1 if forward else -1)) % count
            partner = (other * CORES + core, col) if axis == "row" else (row, other)
            pairs.append((row * cols + col, partner[0] * cols + partner[1]))
    return lax.ppermute(value, axes, pairs)


def shifted(value, axis, steps):
    count = lax.axis_size(axis)
    return lax.ppermute(value, axis, [(source, (source + steps) % count) for source in range(count)])


def siblings(value):
    count = lax.axis_size("row")
    return lax.ppermute(value, "row", [(source, source ^ 1) for source in range(count)])


def body(density_tiles, density_rows, square_tiles, square_cols, keep_rows, keep_cols, square_kept):
    n_row, n_col, n_depth = lax.axis_size("row"), lax.axis_size("col"), lax.axis_size("depth")
    my_row, my_col = lax.axis_index("row"), lax.axis_index("col")
    held_a, blk = density_tiles.shape[3], density_tiles.shape[4]
    pieces, held_b = square_tiles.shape[3], square_tiles.shape[4]
    slots = keep_rows.shape[-1]
    cut = held_b * blk + PAD
    place = jnp.stack([my_row, my_col, lax.axis_index("depth")]).astype(jnp.int32)
    smem = pl.BlockSpec(memory_space=pltpu.SMEM)
    whole = pl.BlockSpec(memory_space=pltpu.VMEM)
    params = pltpu.CompilerParams(vmem_limit_bytes=VMEM_BYTES)
    tile_a, tile_b = pl.pallas_call(
        functools.partial(prepare_kernel, (held_a, held_b, blk, cut, n_col)),
        out_shape=[
            jax.ShapeDtypeStruct((held_a * blk + PAD, blk), jnp.bfloat16),
            jax.ShapeDtypeStruct((cut + held_b * blk, blk), jnp.bfloat16),
        ],
        in_specs=[smem] * 3 + [pl.BlockSpec(memory_space=pl.ANY)] * 2,
        out_specs=[whole] * 2,
        scratch_shapes=[pltpu.SemaphoreType.DMA((3,))],
        compiler_params=pltpu.CompilerParams(vmem_limit_bytes=60 * 1024 * 1024),
        name="prepare",
    )(
        place,
        density_rows[0, 0, 0],
        square_cols[0, 0, 0],
        density_tiles[0, 0, 0].reshape(held_a * blk, blk),
        square_tiles[0, 0, 0].reshape(pieces * held_b * blk, blk),
    )
    tile_a, tile_b = tile_a[None], tile_b[None]

    def swap(value, axis, turn):
        return exchanged(value, ("row", "col"), (n_row, n_col), axis, turn % 2 == 0)

    def both(turn, pair):
        return [swap(pair[0], "row", turn), swap(pair[1], "col", turn)]

    tiles = (tile_a, tile_b)
    first = both(0, tiles)
    second = both(1, tiles)
    second = [jnp.concatenate(two) for two in zip(second, both(1, first))]
    third = both(0, second)
    fourth = both(1, third)
    from_sibling = [
        siblings(jnp.concatenate([tile_a, first[0], second[0]])),
        siblings(third[0]),
        siblings(fourth[0]),
    ]
    chain_a, chain_b = [list(parts) for parts in zip(tiles, first, second, third, fourth)]
    parts_a, parts_b = chain_a + from_sibling, chain_b

    each = slots // n_depth
    sizes = (held_a, held_b, blk, cut)
    coded = jax.ShapeDtypeStruct((each * blk + PAD, blk), jnp.int16)
    summed = (each, blk, blk)

    def cost(count):
        return pl.CostEstimate(flops=8 * count * blk**3, bytes_accessed=count * 2**20, transcendentals=0)

    b_all = pl.pallas_call(
        join_kernel,
        out_shape=jax.ShapeDtypeStruct((n_col + 1, cut + held_b * blk, blk), jnp.bfloat16),
        in_specs=[whole] * len(parts_b),
        out_specs=whole,
        compiler_params=params,
        cost_estimate=pl.CostEstimate(flops=10 * 10**9, bytes_accessed=8 * 2**20, transcendentals=0),
        name="join",
    )(*parts_b)
    far, lists, a_all = pl.pallas_call(
        functools.partial(far_kernel, sizes, n_depth, len(parts_a)),
        out_shape=[
            coded,
            jax.ShapeDtypeStruct((PAD, LANES), jnp.int32),
            jax.ShapeDtypeStruct((n_row, held_a * blk + PAD, blk), jnp.bfloat16),
        ],
        in_specs=[smem] * 3 + [whole] * (len(parts_a) + 1),
        out_specs=[whole] * 3,
        scratch_shapes=[
            pltpu.VMEM(summed, jnp.float32),
            pltpu.SMEM((PAD, LANES), jnp.int32),
            pltpu.SemaphoreType.DMA,
        ],
        compiler_params=params,
        cost_estimate=cost(each),
        name="far",
    )(place, keep_rows[0, 0], keep_cols[0, 0], *parts_a, b_all)
    far = shifted(far, "depth", 2)
    up, down = pl.pallas_call(
        functools.partial(near_kernel, sizes, n_depth, each),
        out_shape=[coded] * 2,
        in_specs=[smem] * 2 + [whole] * 2,
        out_specs=[whole] * 2,
        scratch_shapes=[pltpu.VMEM(summed, jnp.float32)] * 2,
        compiler_params=params,
        cost_estimate=cost(2 * each),
        name="near",
    )(place, lists, a_all, b_all)
    up = shifted(up, "depth", 1)
    down = shifted(down, "depth", -1)
    own = pl.pallas_call(
        functools.partial(own_kernel, sizes, n_depth, each),
        out_shape=jax.ShapeDtypeStruct(summed, jnp.float32),
        in_specs=[smem] * 2 + [whole] * 2,
        out_specs=whole,
        compiler_params=params,
        cost_estimate=cost(each),
        name="own",
    )(place, lists, a_all, b_all)
    result = pl.pallas_call(
        finish_kernel,
        out_shape=jax.ShapeDtypeStruct(summed, jnp.bfloat16),
        compiler_params=params,
        cost_estimate=pl.CostEstimate(flops=2**21, bytes_accessed=3 * 2**20, transcendentals=0),
        name="finish",
    )(far, up, down, own, square_kept[0, 0])
    return result[None, None]


def solution(mesh):
    placed = (
        P("depth", "row", "col", None, None, None),
        P("depth", "row", "col", None),
        P("depth", "row", "col", None, None, None, None),
        P("depth", "row", "col", None, None),
        P("row", "col", None),
        P("row", "col", None),
        P("row", "col", "depth", None, None),
    )
    return jax.shard_map(
        body,
        mesh=mesh,
        in_specs=placed,
        out_specs=P("row", "col", "depth", None, None),
        check_vma=False,
    )
```

```python
import functools

import jax
import jax.numpy as jnp
from jax import lax
from jax.experimental import pallas as pl
from jax.experimental.pallas import tpu as pltpu
from jax.sharding import PartitionSpec as P

GROUP = 4
LEVELS = 32000.0
FINER = 16.0
PAD = 16
VMEM_BYTES = 18 * 1024 * 1024
CORES = 2
LANES = 128


def prepare_kernel(sizes, place, rows, cols, tile_a, tile_b, out_a, out_b, sems):
    held_a, held_b, blk, cut, owners = sizes
    whole_a, piece = held_a * blk, held_b * blk
    my_row, my_col = place[0], place[1]
    copies = [
        pltpu.make_async_copy(tile_a, out_a.at[pl.ds(0, whole_a), :], sems.at[0]),
        pltpu.make_async_copy(tile_b.at[pl.ds(0, piece), :], out_b.at[pl.ds(0, piece), :], sems.at[1]),
        pltpu.make_async_copy(tile_b.at[pl.ds(piece, piece), :], out_b.at[pl.ds(cut, piece), :], sems.at[2]),
    ]
    for copy in copies:
        copy.start()
    lane = lax.broadcasted_iota(jnp.int32, (PAD, blk), 1) & (LANES // 2 - 1)
    spread = jnp.zeros((PAD, blk), jnp.int32)
    for a in range(held_a):
        spread = jnp.where(lane == my_row * held_a + a, rows[a] + 1, spread)
    out_a[pl.ds(whole_a, PAD), :] = spread.astype(jnp.float32).astype(out_a.dtype)
    spread = jnp.zeros((PAD, blk), jnp.int32)
    for index in range(2 * held_b):
        first = (my_col + index // held_b * owners) * held_a + index % held_b
        spread = jnp.where(lane == first, cols[index // held_b, index % held_b] + 1, spread)
    out_b[pl.ds(piece, PAD), :] = spread.astype(jnp.float32).astype(out_b.dtype)
    for copy in copies:
        copy.wait()


def turned(distance, forward, count):
    distance = jnp.where(forward, distance, count - distance) & (count - 1)
    rank = jnp.zeros_like(distance)
    for place, steps in enumerate(arrivals(count)):
        rank = jnp.where(distance == steps % count, place, rank)
    return rank


def arrivals(count):
    order, low, high = [0, 1], 0, 1
    while len(order) < count:
        order += [low - 1, low - 2]
        low -= 2
        if len(order) < count:
            order += [high + 1, high + 2]
            high += 2
    return order


def starts_forward(core, position):
    return lax.rem(core + position, 2) == 0


def listed(rows_seen, cols_seen, keep_rows, keep_cols, my_row, my_col, sizes):
    slots, held_a, held_b, holders, owners = sizes
    chips = holders // CORES
    my_core, my_chip = lax.rem(my_row, CORES), my_row // CORES
    holder = lax.broadcasted_iota(jnp.int32, (8, LANES), 1)
    core, chip = holder & (CORES - 1), (holder // CORES) & (chips - 1)
    forward = ((core + my_chip) & 1) == 0
    rank_a = turned((chip - my_chip + chips) & (chips - 1), forward, chips)
    rank_a = rank_a + jnp.where(core == my_core, 0, chips)
    offset = (holder + my_col - my_row + holders) & (holders - 1)
    owner, piece = offset & (owners - 1), offset // owners
    rank_b = turned((owner - my_col + owners) & (owners - 1), starts_forward(my_core, my_col), owners)
    rank_a, rank_b = rank_a[:1] * held_a, ((rank_b * 2 + piece) * held_b)[:1]
    lane = lax.broadcasted_iota(jnp.int32, (LANES, LANES), 0)
    holder = lax.broadcasted_iota(jnp.int32, (LANES, LANES), 1)
    mine = (lane < holders * held_a) & ((lane // held_a) == holder)
    pick_a = jnp.where(mine, rank_a + (lane & (held_a - 1)) + 1, 0)
    pick_b = jnp.where(mine, rank_b + (lane & (held_a - 1)) + 1, 0)
    before = jnp.where(lane <= holder, 1, 0)

    def numbers(seen, wanted, pick):
        sublane = lax.broadcasted_iota(jnp.int32, seen.shape, 0)
        target = jnp.full(seen.shape, -1, jnp.int32)
        for slot in range(slots):
            target = jnp.where(sublane == slot, wanted[slot] + 1, target)
        hits = jnp.where(seen == target.astype(jnp.float32), 1.0, 0.0).astype(jnp.bfloat16)
        pick = pick.astype(jnp.float32).astype(jnp.bfloat16)
        return jnp.dot(hits, pick, preferred_element_type=jnp.float32)

    number_a = numbers(rows_seen, keep_rows, pick_a)
    number_b = numbers(cols_seen, keep_cols, pick_b)
    both = jnp.where((number_a > 0) & (number_b > 0), 1.0, 0.0)
    before = before.astype(jnp.float32).astype(jnp.bfloat16)
    place = jnp.dot(both.astype(jnp.bfloat16), before, preferred_element_type=jnp.float32)
    code = (number_a - 1.0) + 128.0 * (number_b - 1.0)
    lane = lax.broadcasted_iota(jnp.int32, both.shape, 1)
    count = jnp.sum(both, axis=1, keepdims=True)
    result = jnp.where(lane == LANES - 1, count, 0.0)
    nothing = 128.0 * owners * 2 * held_b
    for at in range(holders):
        value = jnp.sum(jnp.where(place == at + 1.0, both * code, 0.0), axis=1, keepdims=True)
        result = jnp.where(lane == at, jnp.where(count > at, value, nothing), result)
    return result.astype(jnp.int32)


def multiply(sizes, lists, a_all, b_all, first, total):
    held_a, held_b, blk, cut = sizes

    def block_a(code):
        number = code & 127
        return a_all[number // held_a, pl.ds(pl.multiple_of(lax.rem(number, held_a) * blk, blk), blk), :]

    def block_b(code):
        number = code >> 7
        piece, inside = lax.rem(number // held_b, 2), lax.rem(number, held_b)
        return b_all[number // (2 * held_b), pl.ds(pl.multiple_of(piece * cut + inside * blk, PAD), blk), :]

    def grouped(slot, group):
        codes = [lists[slot, group * GROUP + n] for n in range(GROUP)]
        left = jnp.concatenate([block_a(code) for code in codes], axis=1)
        right = jnp.concatenate([block_b(code) for code in codes], axis=0)
        return jnp.dot(left, right, preferred_element_type=jnp.float32)

    count = total.shape[0]
    for index in range(count):
        total[index] = grouped(first + index, 0)
    for index in range(count):
        slot = first + index

        def one_group(group, carry, index=index, slot=slot):
            total[index] += grouped(slot, group)
            return carry

        lax.fori_loop(1, (lists[slot, LANES - 1] + GROUP - 1) // GROUP, one_group, 0)


def encode(total, index, coded, inside, blk, each):
    largest = jnp.maximum(jnp.max(jnp.abs(total[index]), axis=0, keepdims=True), 1e-30)
    power = jnp.ceil(FINER * jnp.log2(largest / LEVELS))
    values = jnp.round(total[index] * jnp.exp2(power * (-1.0 / FINER)))
    coded[pl.ds(inside * blk, blk), :] = values.astype(jnp.int32).astype(jnp.int16)
    return power


def keep_powers(powers, coded, first):
    row = lax.broadcasted_iota(jnp.int32, (PAD, coded.shape[1]), 0)
    value = jnp.zeros(row.shape, jnp.float32)
    for index, power in enumerate(powers):
        value = jnp.where(row == index, power, value)
    coded[pl.ds(first, PAD), :] = value.astype(jnp.int32).astype(jnp.int16)


def target(place, steps, shares, each):
    return lax.rem(place[2] + steps, shares) * each


def join_kernel(*refs):
    parts, whole = refs[:-1], refs[-1]
    at = 0
    for part in parts:
        size = part.shape[0]
        whole[pl.ds(at, size)] = part[...]
        at += size
    blk = whole.shape[2]
    whole[at, pl.ds(0, blk), :] = jnp.zeros((blk, blk), whole.dtype)


def far_kernel(sizes, shares, count_a, place, keep_rows, keep_cols, *rest):
    parts_a, b_all = rest[:count_a], rest[count_a]
    coded, lists, a_all, total, scalar, sem = rest[count_a + 1 :]
    held_a, held_b, blk, cut = sizes
    holders, owners, slots = a_all.shape[0], b_all.shape[0] - 1, keep_rows.shape[0]
    each = slots // shares
    my_row, my_col = place[0], place[1]
    at = 0
    for part in parts_a:
        size = part.shape[0]
        a_all[pl.ds(at, size)] = part[...]
        at += size
    rows_seen = jnp.sum(a_all[:, pl.ds(held_a * blk, PAD), pl.ds(0, LANES)].astype(jnp.float32), axis=0)
    cols_seen = jnp.sum(b_all[pl.ds(0, owners), pl.ds(cut - PAD, PAD), pl.ds(0, LANES)].astype(jnp.float32), axis=0)
    turn = (my_row - my_col + holders) & (holders - 1)
    cols_seen = pltpu.roll(cols_seen, turn * held_a, 1)
    lists[...] = listed(
        rows_seen, cols_seen, keep_rows, keep_cols, my_row, my_col, (slots, held_a, held_b, holders, owners)
    )
    copy = pltpu.make_async_copy(lists, scalar, sem)
    copy.start()
    copy.wait()
    multiply(sizes, scalar, a_all, b_all, target(place, 2, shares, each), total)
    keep_powers([encode(total, index, coded, index, blk, each) for index in range(each)], coded, each * blk)


def near_kernel(sizes, shares, each, place, lists, a_all, b_all, coded_up, coded_down, total_up, total_down):
    blk = sizes[2]
    multiply(sizes, lists, a_all, b_all, target(place, 1, shares, each), total_up)
    multiply(sizes, lists, a_all, b_all, target(place, shares - 1, shares, each), total_down)
    for total, coded in ((total_up, coded_up), (total_down, coded_down)):
        keep_powers([encode(total, index, coded, index, blk, each) for index in range(each)], coded, each * blk)


def decoded(coded, slot, blk, each):
    power = coded[pl.ds(each * blk, PAD), :].astype(jnp.int32).astype(jnp.float32)[slot : slot + 1]
    values = coded[pl.ds(slot * blk, blk), :].astype(jnp.int32).astype(jnp.float32)
    return values * jnp.exp2(power * (1.0 / FINER))


def own_kernel(sizes, shares, each, place, lists, a_all, b_all, far, square_kept, total):
    blk = sizes[2]
    multiply(sizes, lists, a_all, b_all, target(place, 0, shares, each), total)
    for slot in range(each):
        cube = total[slot] + decoded(far, slot, blk, each)
        total[slot] = 3.0 * square_kept[slot].astype(jnp.float32) - 2.0 * cube


def finish_kernel(up, down, rest, out):
    each, blk = rest.shape[0], rest.shape[1]
    for slot in range(each):
        cube = decoded(up, slot, blk, each) + decoded(down, slot, blk, each)
        out[slot] = (rest[slot] - 2.0 * cube).astype(out.dtype)


def exchanged(value, axes, sizes, axis, first):
    rows, cols = sizes
    pairs = []
    for row in range(rows):
        for col in range(cols):
            core, chip = row % CORES, row // CORES
            count, position = (rows // CORES, chip) if axis == "row" else (cols, col)
            forward = ((core + position) % 2 == 0) == first
            other = (position + (1 if forward else -1)) % count
            partner = (other * CORES + core, col) if axis == "row" else (row, other)
            pairs.append((row * cols + col, partner[0] * cols + partner[1]))
    return lax.ppermute(value, axes, pairs)


def shifted(value, axis, steps):
    count = lax.axis_size(axis)
    return lax.ppermute(value, axis, [(source, (source + steps) % count) for source in range(count)])


def siblings(value):
    count = lax.axis_size("row")
    return lax.ppermute(value, "row", [(source, source ^ 1) for source in range(count)])


def body(density_tiles, density_rows, square_tiles, square_cols, keep_rows, keep_cols, square_kept):
    n_row, n_col, n_depth = lax.axis_size("row"), lax.axis_size("col"), lax.axis_size("depth")
    my_row, my_col = lax.axis_index("row"), lax.axis_index("col")
    held_a, blk = density_tiles.shape[3], density_tiles.shape[4]
    pieces, held_b = square_tiles.shape[3], square_tiles.shape[4]
    slots = keep_rows.shape[-1]
    cut = held_b * blk + PAD
    place = jnp.stack([my_row, my_col, lax.axis_index("depth")]).astype(jnp.int32)
    smem = pl.BlockSpec(memory_space=pltpu.SMEM)
    whole = pl.BlockSpec(memory_space=pltpu.VMEM)
    params = pltpu.CompilerParams(vmem_limit_bytes=VMEM_BYTES)
    tile_a, tile_b = pl.pallas_call(
        functools.partial(prepare_kernel, (held_a, held_b, blk, cut, n_col)),
        out_shape=[
            jax.ShapeDtypeStruct((held_a * blk + PAD, blk), jnp.bfloat16),
            jax.ShapeDtypeStruct((cut + held_b * blk, blk), jnp.bfloat16),
        ],
        in_specs=[smem] * 3 + [pl.BlockSpec(memory_space=pl.ANY)] * 2,
        out_specs=[whole] * 2,
        scratch_shapes=[pltpu.SemaphoreType.DMA((3,))],
        compiler_params=pltpu.CompilerParams(vmem_limit_bytes=60 * 1024 * 1024),
        name="prepare",
    )(
        place,
        density_rows[0, 0, 0],
        square_cols[0, 0, 0],
        density_tiles[0, 0, 0].reshape(held_a * blk, blk),
        square_tiles[0, 0, 0].reshape(pieces * held_b * blk, blk),
    )
    tile_a, tile_b = tile_a[None], tile_b[None]

    def swap(value, axis, turn):
        return exchanged(value, ("row", "col"), (n_row, n_col), axis, turn % 2 == 0)

    def both(turn, pair):
        return [swap(pair[0], "row", turn), swap(pair[1], "col", turn)]

    tiles = (tile_a, tile_b)
    first = both(0, tiles)
    second = both(1, tiles)
    second = [jnp.concatenate(two) for two in zip(second, both(1, first))]
    third = both(0, second)
    fourth = both(1, third)
    from_sibling = [
        siblings(jnp.concatenate([tile_a, first[0], second[0]])),
        siblings(third[0]),
        siblings(fourth[0]),
    ]
    chain_a, chain_b = [list(parts) for parts in zip(tiles, first, second, third, fourth)]
    parts_a, parts_b = chain_a + from_sibling, chain_b

    each = slots // n_depth
    sizes = (held_a, held_b, blk, cut)
    coded = jax.ShapeDtypeStruct((each * blk + PAD, blk), jnp.int16)
    summed = (each, blk, blk)

    def cost(count):
        return pl.CostEstimate(flops=8 * count * blk**3, bytes_accessed=count * 2**20, transcendentals=0)

    b_all = pl.pallas_call(
        join_kernel,
        out_shape=jax.ShapeDtypeStruct((n_col + 1, cut + held_b * blk, blk), jnp.bfloat16),
        in_specs=[whole] * len(parts_b),
        out_specs=whole,
        compiler_params=params,
        cost_estimate=pl.CostEstimate(flops=10 * 10**9, bytes_accessed=8 * 2**20, transcendentals=0),
        name="join",
    )(*parts_b)
    far, lists, a_all = pl.pallas_call(
        functools.partial(far_kernel, sizes, n_depth, len(parts_a)),
        out_shape=[
            coded,
            jax.ShapeDtypeStruct((PAD, LANES), jnp.int32),
            jax.ShapeDtypeStruct((n_row, held_a * blk + PAD, blk), jnp.bfloat16),
        ],
        in_specs=[smem] * 3 + [whole] * (len(parts_a) + 1),
        out_specs=[whole] * 3,
        scratch_shapes=[
            pltpu.VMEM(summed, jnp.float32),
            pltpu.SMEM((PAD, LANES), jnp.int32),
            pltpu.SemaphoreType.DMA,
        ],
        compiler_params=params,
        cost_estimate=cost(each),
        name="far",
    )(place, keep_rows[0, 0], keep_cols[0, 0], *parts_a, b_all)
    far = shifted(far, "depth", 2)
    up, down = pl.pallas_call(
        functools.partial(near_kernel, sizes, n_depth, each),
        out_shape=[coded] * 2,
        in_specs=[smem] * 2 + [whole] * 2,
        out_specs=[whole] * 2,
        scratch_shapes=[pltpu.VMEM(summed, jnp.float32)] * 2,
        compiler_params=params,
        cost_estimate=cost(2 * each),
        name="near",
    )(place, lists, a_all, b_all)
    up = shifted(up, "depth", 1)
    down = shifted(down, "depth", -1)
    own = pl.pallas_call(
        functools.partial(own_kernel, sizes, n_depth, each),
        out_shape=jax.ShapeDtypeStruct(summed, jnp.float32),
        in_specs=[smem] * 2 + [whole] * 4,
        out_specs=whole,
        compiler_params=params,
        cost_estimate=cost(each),
        name="own",
    )(place, lists, a_all, b_all, far, square_kept[0, 0])
    result = pl.pallas_call(
        finish_kernel,
        out_shape=jax.ShapeDtypeStruct(summed, jnp.bfloat16),
        compiler_params=params,
        cost_estimate=pl.CostEstimate(flops=2**21, bytes_accessed=3 * 2**20, transcendentals=0),
        name="finish",
    )(up, down, own)
    return result[None, None]


def solution(mesh):
    placed = (
        P("depth", "row", "col", None, None, None),
        P("depth", "row", "col", None),
        P("depth", "row", "col", None, None, None, None),
        P("depth", "row", "col", None, None),
        P("row", "col", None),
        P("row", "col", None),
        P("row", "col", "depth", None, None),
    )
    return jax.shard_map(
        body,
        mesh=mesh,
        in_specs=placed,
        out_specs=P("row", "col", "depth", None, None),
        check_vma=False,
    )
```
